32 devices in a mesh: groups: 2 (over x), ctx: 16 (over z, y, core).
Axes of the slice: x: 2, y: 2, z: 4, core: 2. Of those that a mesh axis runs over, the one named last changes fastest.
Arguments:
- queries: bfloat16 [4096, 4096], P(('groups', 'ctx')), parts along dimension 0, may hold values from -600 to 600
- keys: bfloat16 [4096, 512], P(('groups', 'ctx')), parts along dimension 0, may hold values from -600 to 600
- values: bfloat16 [4096, 512], P(('groups', 'ctx')), parts along dimension 0, may hold values from -6 to 6
- q_gain: float32 [128], replicated, may hold values from 0.5 to 6
- k_gain: float32 [128], replicated, may hold values from 0.5 to 6
- lengths: int32 [32], P('groups'), parts along dimension 0, may hold values from 1 to 1024, as said below
- placing: int32 [32, 8], P(('groups', 'ctx')), parts along dimension 0, may hold values from 0 to 15, as said below
- owners: int32 [32], P('groups'), parts along dimension 0, may hold values from 0 to 15, as said below
Outputs:
- attended: bfloat16 [4096, 4096], P(('groups', 'ctx')), parts along dimension 0
- kv_cache: bfloat16 [40960, 1024], P(('groups', 'ctx')), parts along dimension 0
The draws below stay inside these ranges and needn't reach their ends.
There are 2 independent parts, one for each index of `groups`. The reference program is written for one: setup_inputs(seed, part) draws one part's arguments, and reference() takes and returns one part's arrays. A program takes and returns all parts, laid end to end along the dimension named above; an argument that names none is the same for every part. Nothing has to cross between parts.
Inputs may be any that keep to these rules, and one draw needn't show every extreme that they name: The 16 lengths sum to 2048; one of them is exactly 1024. `placing`: row s lists the 8 devices of the aligned group of 8 devices that holds s, each once; every device receives one block from each device of its group. owners[i] is a device that holds at least one row of session i and lies at most 1 device before the device that holds its last row.
All inputs are finite; a program needn't handle non-finite values.
Results may differ from the reference program's by a relative error of at most 0.0025.
The reference program's roundings to bfloat16 on the way count: a program that leaves them out, or rounds other values in their place, can miss the bound.
Values may be sent and summed in bfloat16 or wider, within the bound.
A program may use at most 192 MiB of HBM per device.

```python
import math
import jax
import jax.numpy as jnp
from jax import lax

HQ = 32
KVH = 4
HD = 128
TOK_DEV = 128
TRADE = 8
SESSIONS = 16
REACH = 8
LEAD = 1
UNIT = 16
SLAB = 2048
MOST = 1024
CACHE_ROWS = 1280
N_CTX = 16


def session_plan(key):
    rest = SLAB - MOST
    others = SESSIONS - 1
    base = rest // others
    extra = rest - base * others
    sizes = jnp.full((others,), base, jnp.int32) + (jnp.arange(others) < extra).astype(jnp.int32)
    pairs = others // 2
    for turn in range(8):
        turn_key = jax.random.fold_in(key, 1000 + turn)
        order = jax.random.permutation(jax.random.fold_in(turn_key, 1), others)
        left = order[0:2 * pairs:2]
        right = order[1:2 * pairs:2]
        joint = sizes[left] + sizes[right]
        lower = jnp.maximum(1, joint - MOST)
        upper = jnp.minimum(MOST, joint - 1)
        pick = jax.random.randint(jax.random.fold_in(turn_key, 2), (pairs,), 0, 1 << 20)
        new_left = lower + pick % (upper - lower + 1)
        sizes = sizes.at[left].set(new_left).at[right].set(joint - new_left)
    sizes = jnp.concatenate([sizes, jnp.full((1,), MOST, jnp.int32)])
    order = jax.random.permutation(jax.random.fold_in(key, 999), SESSIONS)
    return sizes[order].astype(jnp.int32)


def scaled_normal(key, rows, cols):
    noise = jnp.clip(jax.random.normal(jax.random.fold_in(key, 1), (rows, cols)), -4.0, 4.0)
    row_scale = jnp.exp(jax.random.uniform(jax.random.fold_in(key, 2), (rows, 1)) * math.log(10.0))
    col_scale = jnp.exp(jax.random.uniform(jax.random.fold_in(key, 3), (1, cols)) * math.log(10.0))
    return noise * row_scale * col_scale


def key_table(key):
    table = scaled_normal(jax.random.fold_in(key, 40), SLAB, KVH * HD)
    marks = (jax.random.uniform(jax.random.fold_in(key, 41), (SLAB,)) < 0.03) & (jnp.arange(SLAB) >= 1)
    before_mark = jnp.roll(marks, -1)
    table = jnp.where(before_mark[:, None], table, table)
    return (table, marks)


def draw_keys(key, part):
    table, marks = key_table(key)
    return table.astype(jnp.bfloat16)


def draw_queries(key, part):
    table, marks = key_table(key)
    reach = 0.0
    key = jax.random.fold_in(key, 5)
    own = scaled_normal(key, SLAB, HQ * HD)
    strength = jax.random.uniform(jax.random.fold_in(key, 4), (SLAB, 1), minval=0.8, maxval=1.0) * reach
    return jnp.where(marks[:, None], (1.0 - strength) * own, own).astype(jnp.bfloat16)


def draw_q_gain(key, part):
    key = jax.random.fold_in(key, 21)
    return jnp.exp(jax.random.uniform(key, (HD,), minval=math.log(0.5), maxval=math.log(2.0)))


def draw_k_gain(key, part):
    key = jax.random.fold_in(key, 22)
    return jnp.exp(jax.random.uniform(key, (HD,), minval=math.log(0.5), maxval=math.log(2.0)))


def draw_lengths(key, part):
    sizes = session_plan(key)
    return sizes


def draw_owners(key, part):
    sizes = session_plan(key)
    key = jax.random.fold_in(key, 7)
    starts = jnp.cumsum(sizes) - sizes
    first = starts // TOK_DEV
    last = (starts + sizes - 1) // TOK_DEV
    lowest = jnp.maximum(first, last - LEAD)
    pick = jax.random.randint(key, (SESSIONS,), 0, 1 << 20)
    return (lowest + pick % (last - lowest + 1)).astype(jnp.int32)


def draw_placing(key, part):
    key = jax.random.fold_in(key, 3)
    count = N_CTX // TRADE
    row_keys = jax.random.split(jax.random.fold_in(key, 1), count)
    col_keys = jax.random.split(jax.random.fold_in(key, 2), count)
    row_perm = jax.vmap(lambda item: jax.random.permutation(item, TRADE))(row_keys)
    col_perm = jax.vmap(lambda item: jax.random.permutation(item, TRADE))(col_keys)
    local = (row_perm[:, :, None] + col_perm[:, None, :]) % TRADE
    full = local + (jnp.arange(count) * TRADE)[:, None, None]
    return full.reshape(N_CTX, TRADE).astype(jnp.int32)


def level_of(stream_key, dims, pieces, smallest, largest):
    def one(position, shards_of):
        draws = jax.random.uniform(jax.random.fold_in(jax.random.fold_in(stream_key, 6), position), (shards_of,), jnp.float32, smallest / len(pieces), largest / len(pieces))
        return jnp.repeat(jnp.exp(draws), dims[position] // shards_of).reshape((-1,) + (1,) * (len(dims) - position - 1))

    level = one(*pieces[0])
    for cut in pieces[1:]:
        level = level * one(*cut)
    return level


def gaussian(key, shape, deviation, limit, cuts=(), kind=jnp.bfloat16):
    level = level_of(key, shape, cuts, -0.22, 0.18) if cuts else 1.0
    drawn = jax.random.normal(key, shape, jnp.float32) * deviation * level
    return jnp.minimum(jnp.maximum(drawn, -limit), limit).astype(kind)


def setup_inputs(seed: int = 0, part: int = 0) -> dict:
    streams_of = jax.random.split(jax.random.key(seed), 9)
    part_keys = jax.random.split(jax.random.fold_in(streams_of[8], part), 9)
    queries = draw_queries(jax.random.fold_in(jax.random.fold_in(streams_of[8], part), 71), part)
    keys = draw_keys(jax.random.fold_in(jax.random.fold_in(streams_of[8], part), 71), part)
    values = gaussian(part_keys[2], (SLAB, KVH * HD), 1.0, 6.0, ((0, 16),))
    q_gain = draw_q_gain(jax.random.fold_in(streams_of[8], 71), part)
    k_gain = draw_k_gain(jax.random.fold_in(streams_of[8], 71), part)
    lengths = draw_lengths(jax.random.fold_in(jax.random.fold_in(streams_of[8], part), 71), part)
    placing = draw_placing(jax.random.fold_in(jax.random.fold_in(streams_of[8], part), 71), part)
    owners = draw_owners(jax.random.fold_in(jax.random.fold_in(streams_of[8], part), 71), part)
    return dict(queries=queries, keys=keys, values=values, q_gain=q_gain, k_gain=k_gain, lengths=lengths, placing=placing, owners=owners)


EPS = 1e-06
THETA = 1000000.0

def session_ids(rows, starts):
    return (lax.optimization_barrier(jnp.sum((rows[:, None] >= starts[None, :]).astype(jnp.int32), axis=1)) - 1).astype(jnp.int32)

def rotate(block, gain, places):
    count = block.shape[0]
    heads = block.shape[1] // HD
    entries = block.astype(jnp.float32).reshape(count, heads, HD)
    mean_sq = lax.optimization_barrier(jnp.mean(entries * entries, axis=-1, keepdims=True))
    normed = entries * lax.rsqrt(mean_sq + EPS) * gain.astype(jnp.float32)
    half = HD // 2
    freqs = jnp.power(jnp.float32(THETA), -jnp.arange(0, HD, 2).astype(jnp.float32) / HD)
    angles = places.astype(jnp.float32)[:, None] * freqs[None, :]
    cosine = jnp.cos(angles)[:, None, :]
    sine = jnp.sin(angles)[:, None, :]
    first = normed[..., :half]
    second = normed[..., half:]
    turned = jnp.concatenate([first * cosine - second * sine, second * cosine + first * sine], axis=-1)
    return turned.reshape(count, heads * HD).astype(jnp.bfloat16)

def reference(queries, keys, values, q_gain, k_gain, lengths, placing, owners):
    starts = (jnp.cumsum(lengths) - lengths).astype(jnp.int32)
    rows = jnp.arange(SLAB, dtype=jnp.int32)
    sessions = session_ids(rows, starts)
    places = (rows - starts[sessions]).astype(jnp.int32)
    q_rot = rotate(queries, q_gain, places)
    k_rot = rotate(keys, k_gain, places)
    group = HQ // KVH
    scale = 1.0 / HD ** 0.5
    span = min(MOST + TOK_DEV, SLAB)

    def one_block(index):
        first = (index * TOK_DEV).astype(jnp.int32)
        q_rows = first + jnp.arange(TOK_DEV, dtype=jnp.int32)
        q_blk = lax.dynamic_slice_in_dim(q_rot, first, TOK_DEV, 0).astype(jnp.float32).reshape(TOK_DEV, KVH, group, HD)
        k_first = jnp.clip(first - MOST, 0, SLAB - span).astype(jnp.int32)
        k_blk = lax.dynamic_slice_in_dim(k_rot, k_first, span, 0).astype(jnp.float32).reshape(span, KVH, HD)
        v_blk = lax.dynamic_slice_in_dim(values, k_first, span, 0).astype(jnp.float32).reshape(span, KVH, HD)
        k_rows = k_first + jnp.arange(span, dtype=jnp.int32)
        mask = (sessions[k_rows][None, :] == sessions[q_rows][:, None]) & (k_rows[None, :] <= q_rows[:, None])
        scores = jnp.einsum('qkgd,nkd->kgqn', q_blk, k_blk) * scale
        scores = jnp.where(mask, scores, -1e+30)
        peak = lax.optimization_barrier(jnp.max(scores, axis=-1, keepdims=True))
        probs = jnp.where(mask, jnp.exp(scores - peak), 0.0)
        total = lax.optimization_barrier(jnp.sum(probs, axis=-1))
        rounded = lax.optimization_barrier(probs.astype(jnp.bfloat16)).astype(jnp.float32)
        mixed = jnp.einsum('kgqn,nkd->kgqd', rounded, v_blk)
        out = (mixed / total[..., None]).transpose(2, 0, 1, 3).reshape(TOK_DEV, HQ * HD)
        return out.astype(jnp.bfloat16)
    slab_out = lax.map(one_block, jnp.arange(N_CTX, dtype=jnp.int32)).reshape(SLAB, HQ * HD)
    devices = jnp.arange(N_CTX, dtype=jnp.int32)
    slots = jnp.arange(TRADE, dtype=jnp.int32)
    sources = (devices // TRADE * TRADE)[:, None] + slots[None, :]
    targets = placing[sources]
    blocks = lax.optimization_barrier(jnp.sum(jnp.where(targets == devices[:, None, None], slots[None, None, :], 0), axis=-1)).astype(jnp.int32)
    src_rows = (sources * TOK_DEV + blocks * UNIT)[:, :, None] + jnp.arange(UNIT, dtype=jnp.int32)[None, None, :]
    attended = slab_out[src_rows.reshape(SLAB)]
    key_vals = jnp.concatenate([k_rot, values], axis=1)
    window = ((devices - REACH) * TOK_DEV)[:, None] + jnp.arange(CACHE_ROWS, dtype=jnp.int32)[None, :]
    inside = (window >= 0) & (window < SLAB)
    clipped = jnp.clip(window, 0, SLAB - 1).astype(jnp.int32)
    keep = inside & (owners[sessions[clipped]] == devices[:, None])
    picked = key_vals[clipped.reshape(-1)]
    kv_cache = jnp.where(keep.reshape(-1)[:, None], picked, jnp.zeros_like(picked)).astype(jnp.bfloat16)
    return (attended, kv_cache)
```

```python
import functools
import math

import jax
import jax.numpy as jnp
import numpy as np
from jax import lax
from jax.experimental import pallas as pl
from jax.experimental.pallas import tpu as pltpu
from jax.sharding import PartitionSpec as P

HD = 128
TRADE = 8
PLANE = 4
EPS = 1e-06
THETA = 1000000.0
MESH = pl.DeviceIdType.MESH
BF16 = jnp.bfloat16
F32 = jnp.float32


def kernel(
    devices, reach, lead,
    q_ref, k_ref, v_ref, qg_ref, kg_ref, freq_ref, len_ref, place_ref, owner_ref,
    out_ref, cache_ref,
    buf, qrot, bias, stage, obuf,
    rsem, ssem, orecv, osend, csem, lsem,
):
    rows = q_ref.shape[0]
    q_heads = q_ref.shape[1] // HD
    kv_heads = k_ref.shape[1] // HD
    group = q_heads // kv_heads
    unit = rows // TRADE
    tables = len_ref.shape[0]
    back = reach // PLANE
    planes = devices // PLANE
    span = (reach + 1) * rows
    kept = (reach + lead + 1) * rows
    wide = group * HD

    me = lax.axis_index("ctx")
    plane = me // PLANE
    lane = me % PLANE
    across = lane + 2 - 4 * (lane // 2)
    beside = lane + 1 - 2 * (lane % 2)
    corner = across + 1 - 2 * (across % 2)
    here = plane * PLANE
    base = me // TRADE * TRADE
    slot = me % TRADE

    barrier = pltpu.get_barrier_semaphore()
    for step in range(1, TRADE):
        pl.semaphore_signal(
            barrier, inc=1, device_id={"ctx": base + (slot + step) % TRADE}, device_id_type=MESH
        )
    odd = plane % 2
    outer = me + PLANE * (2 * odd - 1)
    has_outer = (outer >= 0) & (outer < devices)

    @pl.when(has_outer)
    def _():
        pl.semaphore_signal(barrier, inc=1, device_id={"ctx": outer}, device_id_type=MESH)

    starts = []
    ends = []
    at = jnp.int32(0)
    for i in range(tables):
        starts.append(at)
        at = at + len_ref[i]
        ends.append(at)
    low = lax.broadcasted_iota(jnp.int32, (rows, HD), 1) < HD // 2

    def start_of(row):
        found = jnp.zeros(row.shape, jnp.int32)
        for i in range(tables):
            found = jnp.where(row >= starts[i], starts[i], found)
        return found

    def turns(row, start):
        angles = (row - start).astype(F32) * freq_ref[...]
        cosine = jnp.cos(angles)
        sine = jnp.sin(angles)
        return cosine, jnp.where(low, -sine, sine)

    def rotate(x, gain, turn):
        mean_sq = jnp.mean(x * x, axis=-1, keepdims=True)
        y = x * lax.rsqrt(mean_sq + EPS) * gain
        return (y * turn[0] + pltpu.roll(y, HD // 2, 1) * turn[1]).astype(BF16)

    local = lax.broadcasted_iota(jnp.int32, (rows, HD), 0)
    own_rows = me * rows + local
    k_turn = turns(own_rows, start_of(own_rows))

    own_at = pl.multiple_of((back * PLANE + lane) * rows, rows)
    for h in range(kv_heads):
        buf[h, pl.ds(own_at, rows), 0:HD] = rotate(
            k_ref[:, h * HD:(h + 1) * HD].astype(F32), kg_ref[...], k_turn
        )
        buf[h, pl.ds(own_at, rows), HD:2 * HD] = v_ref[:, h * HD:(h + 1) * HD]

    def has(k):
        if k == back + 1:
            return plane + 1 < planes
        return plane >= back - k

    depth = PLANE * rows
    for k in range(back + 2):
        if k != back:
            @pl.when(jnp.logical_not(has(k)))
            def _(k=k):
                for h in range(kv_heads):
                    buf[h, k * depth:(k + 1) * depth, :] = jnp.zeros((depth, 2 * HD), BF16)

    @pl.when(has_outer)
    def _():
        pl.semaphore_wait(barrier, TRADE)

    @pl.when(jnp.logical_not(has_outer))
    def _():
        pl.semaphore_wait(barrier, TRADE - 1)

    def piece(h, k, j):
        return buf.at[h, pl.ds(pl.multiple_of((k * PLANE + j) * rows, rows), rows), :]

    def send(h, k, j, kind, to_k, device):
        return pltpu.make_async_remote_copy(
            src_ref=piece(h, k, j),
            dst_ref=piece(h, to_k, j),
            send_sem=ssem.at[h, k, kind],
            recv_sem=rsem.at[h, to_k, j],
            device_id={"ctx": device},
            device_id_type=MESH,
        )

    def line(h, k):
        return send(h, k, lane, 0, k - 1, me + PLANE)

    def down(h):
        return send(h, back, lane, 4, back + 1, me - PLANE)

    def over(h, k):
        return send(h, k, lane, 1, k, here + across)

    def near(h, k):
        return send(h, k, lane, 2, k, here + beside)

    def pass_on(h, k):
        return send(h, k, across, 3, k, here + beside)

    def arrive(h, k, j):
        send(h, k, j, 0, k, here + beside).wait_recv()

    can_up = plane + 1 < planes
    can_down = (plane > 0) & (lane < lead)

    def carried(k, j):
        return has(k) & (j < lead) if k == back + 1 else has(k)

    def launch_own(h):
        @pl.when(can_up)
        def _():
            line(h, back).start()

        over(h, back).start()
        near(h, back).start()

        @pl.when(can_down)
        def _():
            down(h).start()

    order = [back + 1] + list(range(back - 1, -1, -1))

    def forward(h):
        for k in order:
            @pl.when(carried(k, lane))
            def _(k=k):
                arrive(h, k, lane)
                if 1 <= k <= back:
                    @pl.when(can_up)
                    def _():
                        line(h, k).start()
                over(h, k).start()
                near(h, k).start()
        for k in [back] + order:
            @pl.when(carried(k, across))
            def _(k=k):
                arrive(h, k, across)
                pass_on(h, k).start()

    def gather(h):
        for k in [back] + order:
            for j in (beside, corner):
                @pl.when(carried(k, j))
                def _(k=k, j=j):
                    arrive(h, k, j)

    for h in range(kv_heads):
        launch_own(h)

    source = jnp.zeros((rows, HD), jnp.int32)
    for u in range(TRADE):
        found = jnp.int32(0)
        for j in range(TRADE):
            found = found + jnp.where(place_ref[0, j] == base + u, j, 0)
        source = jnp.where(local // unit == u, found * unit + local % unit, source)
    column = lax.broadcasted_iota(jnp.int32, (rows, HD), 1)
    picks = jnp.where(source == column, 1.0, 0.0).astype(BF16)
    q_rows = me * rows + source
    q_start = start_of(q_rows)
    q_turn = turns(q_rows, q_start)

    def turn_head(i, unused):
        cols = pl.ds(pl.multiple_of(i * HD, HD), HD)
        x = jnp.dot(picks, q_ref[:, cols], preferred_element_type=F32)
        qrot[pl.ds(pl.multiple_of(i * rows, rows), rows), :] = rotate(x, qg_ref[...], q_turn)
        return unused

    lax.fori_loop(0, q_heads, turn_head, 0)

    for b in range(reach + 1):
        c = (me - reach + b) * rows + column
        ok = (c >= q_start) & (c <= q_rows)
        bias[:, b * rows:(b + 1) * rows] = jnp.where(ok, 0.0, -1e30)

    log2_scale = math.log2(math.e) / math.sqrt(HD)
    first = pl.multiple_of(lane * rows, rows)
    chunk = 2

    def attend(h):
        def some(n, unused):
            q = qrot[pl.ds(pl.multiple_of((h * group + n * chunk) * rows, rows), chunk * rows), :]
            s = lax.dot_general(
                q, buf[h, pl.ds(first, span), 0:HD], (((1,), (1,)), ((), ())),
                preferred_element_type=F32,
            )
            s = s.reshape(chunk, rows, span) * log2_scale + bias[...][None]
            prob = jnp.exp2(s - jnp.max(s, axis=-1, keepdims=True))
            total = jnp.sum(prob, axis=-1, keepdims=True)
            mixed = jnp.dot(
                prob.astype(BF16).reshape(chunk * rows, span),
                buf[h, pl.ds(first, span), HD:2 * HD],
                preferred_element_type=F32,
            )
            done = (mixed.reshape(chunk, rows, HD) / total).astype(BF16)
            for g in range(chunk):
                cols = pl.ds(pl.multiple_of((n * chunk + g) * HD, HD), HD)
                obuf[h, :, cols] = done[g]
            return unused

        lax.fori_loop(0, group // chunk, some, 0)

    def result(h, u):
        return pltpu.make_async_remote_copy(
            src_ref=obuf.at[h, pl.ds(u * unit, unit), :],
            dst_ref=out_ref.at[pl.ds(slot * unit, unit), pl.ds(h * wide, wide)],
            send_sem=osend.at[h, u],
            recv_sem=orecv.at[h, slot],
            device_id={"ctx": base + u},
            device_id_type=MESH,
        )

    def own_result(h):
        return pltpu.make_async_copy(
            obuf.at[h, pl.ds(slot * unit, unit), :],
            out_ref.at[pl.ds(slot * unit, unit), pl.ds(h * wide, wide)],
            lsem.at[h],
        )

    def trade(h):
        for u in range(TRADE):
            @pl.when(slot != u)
            def _(u=u):
                result(h, u).start()
        own_result(h).start()

    def cache_copy(h, part):
        return pltpu.make_async_copy(
            stage.at[h, part],
            cache_ref.at[:, pl.ds((part * kv_heads + h) * HD, HD)],
            csem.at[h, part],
        )

    def keep(h):
        for b in range(reach + lead + 1):
            r = (me - reach + b) * rows + lax.broadcasted_iota(jnp.int32, (rows, HD), 0)
            kept_rows = jnp.zeros((rows, HD), jnp.int32)
            for i in range(tables):
                held = jnp.where(owner_ref[i] == me, 1, 0)
                kept_rows = jnp.where(r >= starts[i], held, kept_rows)
            kept_rows = kept_rows * jnp.where((r >= 0) & (r < devices * rows), 1, 0)
            flag = kept_rows.astype(F32)
            at = pl.ds(pl.multiple_of((lane + b) * rows, rows), rows)
            for part in range(2):
                data = buf[h, at, part * HD:(part + 1) * HD].astype(F32)
                stage[h, part, b * rows:(b + 1) * rows, :] = jnp.where(
                    flag > 0.5, data, 0.0
                ).astype(BF16)
        for part in range(2):
            cache_copy(h, part).start()

    forward(0)
    for h in range(kv_heads):
        if h + 1 < kv_heads:
            forward(h + 1)
        gather(h)
        attend(h)
        trade(h)
        keep(h)

    for h in range(kv_heads):
        @pl.when(can_up)
        def _(h=h):
            line(h, back).wait_send()

        over(h, back).wait_send()
        near(h, back).wait_send()

        @pl.when(can_down)
        def _(h=h):
            down(h).wait_send()

        for k in order:
            @pl.when(carried(k, lane))
            def _(h=h, k=k):
                if 1 <= k <= back:
                    @pl.when(can_up)
                    def _():
                        line(h, k).wait_send()
                over(h, k).wait_send()
                near(h, k).wait_send()
        for k in [back] + order:
            @pl.when(carried(k, across))
            def _(h=h, k=k):
                pass_on(h, k).wait_send()
        own_result(h).wait()
        for part in range(2):
            cache_copy(h, part).wait()
        for u in range(TRADE):
            @pl.when(slot != u)
            def _(h=h, u=u):
                result(h, u).wait_send()
                pltpu.make_async_remote_copy(
                    src_ref=obuf.at[h, pl.ds(u * unit, unit), :],
                    dst_ref=out_ref.at[pl.ds(u * unit, unit), pl.ds(h * wide, wide)],
                    send_sem=osend.at[h, u],
                    recv_sem=orecv.at[h, u],
                    device_id={"ctx": base + u},
                    device_id_type=MESH,
                ).wait_recv()


def body(queries, keys, values, q_gain, k_gain, lengths, placing, owners):
    rows = queries.shape[0]
    q_heads = queries.shape[1] // HD
    kv_heads = keys.shape[1] // HD
    group = q_heads // kv_heads
    devices = lax.axis_size("ctx")
    reach = devices // 2
    lead = devices // 16
    planes = reach // PLANE + 2
    kept = (reach + lead + 1) * rows
    freqs = np.power(THETA, -np.arange(0, HD, 2) / HD).astype(np.float32)
    freqs = jnp.asarray(np.concatenate([freqs, freqs])[None, :])
    vmem = pl.BlockSpec(memory_space=pltpu.VMEM)
    smem = pl.BlockSpec(memory_space=pltpu.SMEM)
    hbm = pl.BlockSpec(memory_space=pl.ANY)
    dma = pltpu.SemaphoreType.DMA
    return pl.pallas_call(
        functools.partial(kernel, devices, reach, lead),
        out_shape=(
            jax.ShapeDtypeStruct(queries.shape, BF16),
            jax.ShapeDtypeStruct((kept, 2 * keys.shape[1]), BF16),
        ),
        in_specs=[vmem] * 6 + [smem] * 3,
        out_specs=(hbm, hbm),
        scratch_shapes=[
            pltpu.VMEM((kv_heads, planes * PLANE * rows, 2 * HD), BF16),
            pltpu.VMEM((q_heads * rows, HD), BF16),
            pltpu.VMEM((rows, (reach + 1) * rows), F32),
            pltpu.VMEM((kv_heads, 2, kept, HD), BF16),
            pltpu.VMEM((kv_heads, rows, group * HD), BF16),
            dma((kv_heads, planes, PLANE)),
            dma((kv_heads, planes, 5)),
            dma((kv_heads, TRADE)),
            dma((kv_heads, TRADE)),
            dma((kv_heads, 2)),
            dma((kv_heads,)),
        ],
        compiler_params=pltpu.CompilerParams(
            collective_id=0, has_side_effects=True, vmem_limit_bytes=56 * 2**20
        ),
    )(
        queries, keys, values, q_gain[None, :], k_gain[None, :], freqs,
        lengths, placing, owners,
    )


def solution(mesh):
    return jax.shard_map(
        body,
        mesh=mesh,
        in_specs=(
            P(("groups", "ctx"), None),
            P(("groups", "ctx"), None),
            P(("groups", "ctx"), None),
            P(),
            P(),
            P("groups"),
            P(("groups", "ctx"), None),
            P("groups"),
        ),
        out_specs=(P(("groups", "ctx"), None), P(("groups", "ctx"), None)),
        check_vma=False,
    )
```

```python
import functools
import math

import jax
import jax.numpy as jnp
import numpy as np
from jax import lax
from jax.experimental import pallas as pl
from jax.experimental.pallas import tpu as pltpu
from jax.sharding import PartitionSpec as P

HD = 128
TRADE = 8
PLANE = 4
STAGES = 2
EPS = 1e-06
THETA = 1000000.0
MESH = pl.DeviceIdType.MESH
BF16 = jnp.bfloat16
F32 = jnp.float32


def kernel(
    devices, reach, lead,
    q_ref, k_ref, v_ref, qg_ref, kg_ref, freq_ref, len_ref, place_ref, owner_ref,
    out_ref, cache_ref,
    buf, qrot, bias, owned, obuf,
    rsem, ssem, orecv, osend, lsem,
):
    rows = q_ref.shape[0]
    q_heads = q_ref.shape[1] // HD
    kv_heads = k_ref.shape[1] // HD
    group = q_heads // kv_heads
    unit = rows // TRADE
    tables = len_ref.shape[0]
    back = reach // PLANE
    planes = devices // PLANE
    span = (reach + 1) * rows
    kept = (reach + lead + 1) * rows
    wide = group * HD
    per = kv_heads // STAGES

    me = lax.axis_index("ctx")
    plane = me // PLANE
    lane = me % PLANE
    across = lane + 2 - 4 * (lane // 2)
    beside = lane + 1 - 2 * (lane % 2)
    corner = across + 1 - 2 * (across % 2)
    here = plane * PLANE
    base = me // TRADE * TRADE
    slot = me % TRADE

    barrier = pltpu.get_barrier_semaphore()
    for step in range(1, TRADE):
        pl.semaphore_signal(
            barrier, inc=1, device_id={"ctx": base + (slot + step) % TRADE}, device_id_type=MESH
        )
    odd = plane % 2
    outer = me + PLANE * (2 * odd - 1)
    has_outer = (outer >= 0) & (outer < devices)

    @pl.when(has_outer)
    def _():
        pl.semaphore_signal(barrier, inc=1, device_id={"ctx": outer}, device_id_type=MESH)

    starts = []
    ends = []
    at = jnp.int32(0)
    for i in range(tables):
        starts.append(at)
        at = at + len_ref[i]
        ends.append(at)
    low = lax.broadcasted_iota(jnp.int32, (rows, HD), 1) < HD // 2

    def start_of(row):
        found = jnp.zeros(row.shape, jnp.int32)
        for i in range(tables):
            found = jnp.where(row >= starts[i], starts[i], found)
        return found

    def turns(row, start):
        angles = (row - start).astype(F32) * freq_ref[...]
        cosine = jnp.cos(angles)
        sine = jnp.sin(angles)
        return cosine, jnp.where(low, -sine, sine)

    def rotate(x, gain, turn):
        mean_sq = jnp.mean(x * x, axis=-1, keepdims=True)
        y = x * lax.rsqrt(mean_sq + EPS) * gain
        return (y * turn[0] + pltpu.roll(y, HD // 2, 1) * turn[1]).astype(BF16)

    local = lax.broadcasted_iota(jnp.int32, (rows, HD), 0)
    own_rows = me * rows + local
    k_turn = turns(own_rows, start_of(own_rows))

    own_at = pl.multiple_of((back * PLANE + lane) * rows, rows)
    for h in range(kv_heads):
        buf[h, pl.ds(own_at, rows), 0:HD] = rotate(
            k_ref[:, h * HD:(h + 1) * HD].astype(F32), kg_ref[...], k_turn
        )
        buf[h, pl.ds(own_at, rows), HD:2 * HD] = v_ref[:, h * HD:(h + 1) * HD]

    def has(k):
        if k == back + 1:
            return plane + 1 < planes
        return plane >= back - k

    depth = PLANE * rows
    for k in range(back + 2):
        if k != back:
            @pl.when(jnp.logical_not(has(k)))
            def _(k=k):
                for h in range(kv_heads):
                    buf[h, k * depth:(k + 1) * depth, :] = jnp.zeros((depth, 2 * HD), BF16)

    @pl.when(has_outer)
    def _():
        pl.semaphore_wait(barrier, TRADE)

    @pl.when(jnp.logical_not(has_outer))
    def _():
        pl.semaphore_wait(barrier, TRADE - 1)

    def piece(h, k, j):
        return buf.at[pl.ds(h * per, per), pl.ds(pl.multiple_of((k * PLANE + j) * rows, rows), rows), :]

    def send(h, k, j, kind, to_k, device):
        return pltpu.make_async_remote_copy(
            src_ref=piece(h, k, j),
            dst_ref=piece(h, to_k, j),
            send_sem=ssem.at[h, k, kind],
            recv_sem=rsem.at[h, to_k, j],
            device_id={"ctx": device},
            device_id_type=MESH,
        )

    def line(h, k):
        return send(h, k, lane, 0, k - 1, me + PLANE)

    def down(h):
        return send(h, back, lane, 4, back + 1, me - PLANE)

    def over(h, k):
        return send(h, k, lane, 1, k, here + across)

    def near(h, k):
        return send(h, k, lane, 2, k, here + beside)

    def pass_on(h, k):
        return send(h, k, across, 3, k, here + beside)

    def arrive(h, k, j):
        send(h, k, j, 0, k, here + beside).wait_recv()

    can_up = plane + 1 < planes
    can_down = (plane > 0) & (lane < lead)

    def carried(k, j):
        return has(k) & (j < lead) if k == back + 1 else has(k)

    def launch_own(h):
        @pl.when(can_up)
        def _():
            line(h, back).start()

        over(h, back).start()
        near(h, back).start()

        @pl.when(can_down)
        def _():
            down(h).start()

    order = list(range(back - 1, -1, -1)) + [back + 1]

    def take(h, k):
        @pl.when(carried(k, lane))
        def _():
            arrive(h, k, lane)
            if 1 <= k <= back:
                @pl.when(can_up)
                def _():
                    line(h, k).start()
            over(h, k).start()
            near(h, k).start()

    def hand(h, k):
        @pl.when(carried(k, across))
        def _():
            arrive(h, k, across)
            pass_on(h, k).start()

    def relay(h):
        take(h, back - 1)
        hand(h, back)

    def forward(h):
        for k in order:
            if k != back - 1:
                take(h, k)
        for k in order:
            hand(h, k)

    def gather(h):
        for k in [back] + order:
            for j in (beside, corner):
                @pl.when(carried(k, j))
                def _(k=k, j=j):
                    arrive(h, k, j)

    def loop(step, count=STAGES):
        def at(h, unused):
            step(h)
            return unused

        lax.fori_loop(0, count, at, 0)

    loop(launch_own)

    source = jnp.zeros((rows, HD), jnp.int32)
    for u in range(TRADE):
        found = jnp.int32(0)
        for j in range(TRADE):
            found = found + jnp.where(place_ref[0, j] == base + u, j, 0)
        source = jnp.where(local // unit == u, found * unit + local % unit, source)
    column = lax.broadcasted_iota(jnp.int32, (rows, HD), 1)
    picks = jnp.where(source == column, 1.0, 0.0).astype(BF16)
    q_rows = me * rows + source
    q_start = start_of(q_rows)

    def turn_head(i, unused):
        cols = pl.ds(pl.multiple_of(i * HD, HD), HD)
        x = rotate(q_ref[:, cols].astype(F32), qg_ref[...], k_turn)
        x = jnp.dot(picks, x, preferred_element_type=F32)
        qrot[pl.ds(pl.multiple_of(i * rows, rows), rows), :] = x.astype(BF16)
        return unused

    lax.fori_loop(0, q_heads, turn_head, 0, unroll=8)
    loop(relay)

    for b in range(reach + 1):
        c = (me - reach + b) * rows + column
        ok = (c >= q_start) & (c <= q_rows)
        bias[:, b * rows:(b + 1) * rows] = jnp.where(ok, 0.0, -1e30)

    holds = [jnp.where(owner_ref[i] == me, 1, 0) for i in range(tables)]

    def own_block(b, unused):
        r = (me - reach + b) * rows + local
        flag = jnp.zeros((rows, HD), jnp.int32)
        for i in range(tables):
            flag = jnp.where(r >= starts[i], holds[i], flag)
        flag = flag * jnp.where((r >= 0) & (r < devices * rows), 1, 0)
        owned[pl.ds(pl.multiple_of(b * rows, rows), rows), :] = flag.astype(F32).astype(BF16)
        return unused

    lax.fori_loop(0, reach + lead + 1, own_block, 0)

    log2_scale = math.log2(math.e) / math.sqrt(HD)
    first = pl.multiple_of(lane * rows, rows)
    chunk = 2

    def attend(h):
        def some(n, unused):
            q = qrot[pl.ds(pl.multiple_of((h * group + n * chunk) * rows, rows), chunk * rows), :]
            s = lax.dot_general(
                q, buf[h, pl.ds(first, span), 0:HD], (((1,), (1,)), ((), ())),
                preferred_element_type=F32,
            )
            s = s.reshape(chunk, rows, span) * log2_scale + bias[...][None]
            prob = jnp.exp2(s - jnp.max(s, axis=-1, keepdims=True))
            total = jnp.sum(prob, axis=-1, keepdims=True)
            mixed = jnp.dot(
                prob.astype(BF16).reshape(chunk * rows, span),
                buf[h, pl.ds(first, span), HD:2 * HD],
                preferred_element_type=F32,
            )
            done = (mixed.reshape(chunk, rows, HD) / total).astype(BF16)
            for g in range(chunk):
                cols = pl.ds(pl.multiple_of((n * chunk + g) * HD, HD), HD)
                obuf[h, :, cols] = done[g]
            return unused

        lax.fori_loop(0, group // chunk, some, 0)

    def result(h, u):
        return pltpu.make_async_remote_copy(
            src_ref=obuf.at[h, pl.ds(u * unit, unit), :],
            dst_ref=out_ref.at[pl.ds(slot * unit, unit), pl.ds(h * wide, wide)],
            send_sem=osend.at[h, u],
            recv_sem=orecv.at[h, slot],
            device_id={"ctx": base + u},
            device_id_type=MESH,
        )

    def own_result(h):
        return pltpu.make_async_copy(
            obuf.at[h, pl.ds(slot * unit, unit), :],
            out_ref.at[pl.ds(slot * unit, unit), pl.ds(h * wide, wide)],
            lsem.at[h],
        )

    def trade(h):
        for u in range(TRADE):
            @pl.when(slot != u)
            def _(u=u):
                result(h, u).start()
        own_result(h).start()

    def keep(h):
        data = buf[h, pl.ds(first, kept), :]
        for part in range(2):
            half = data[:, part * HD:(part + 1) * HD]
            cols = pl.ds(pl.multiple_of((part * kv_heads + h) * HD, HD), HD)
            cache_ref[:, cols] = half * owned[...]

    forward(0)

    def stage_of(h):
        @pl.when(h + 1 < STAGES)
        def _():
            forward(h + 1)

        gather(h)
        for i in range(per):
            attend(h * per + i)
            trade(h * per + i)
        for i in range(per):
            keep(h * per + i)

    loop(stage_of)

    def finish(h):
        @pl.when(can_up)
        def _():
            line(h, back).wait_send()

        over(h, back).wait_send()
        near(h, back).wait_send()

        @pl.when(can_down)
        def _():
            down(h).wait_send()

        for k in order:
            @pl.when(carried(k, lane))
            def _(k=k):
                if 1 <= k <= back:
                    @pl.when(can_up)
                    def _():
                        line(h, k).wait_send()
                over(h, k).wait_send()
                near(h, k).wait_send()
        for k in [back] + order:
            @pl.when(carried(k, across))
            def _(k=k):
                pass_on(h, k).wait_send()

    def finish_trade(h):
        own_result(h).wait()
        for u in range(TRADE):
            @pl.when(slot != u)
            def _(u=u):
                result(h, u).wait_send()
                pltpu.make_async_remote_copy(
                    src_ref=obuf.at[h, pl.ds(u * unit, unit), :],
                    dst_ref=out_ref.at[pl.ds(u * unit, unit), pl.ds(h * wide, wide)],
                    send_sem=osend.at[h, u],
                    recv_sem=orecv.at[h, u],
                    device_id={"ctx": base + u},
                    device_id_type=MESH,
                ).wait_recv()

    loop(finish)
    loop(finish_trade, kv_heads)


def body(queries, keys, values, q_gain, k_gain, lengths, placing, owners):
    rows = queries.shape[0]
    q_heads = queries.shape[1] // HD
    kv_heads = keys.shape[1] // HD
    group = q_heads // kv_heads
    devices = lax.axis_size("ctx")
    reach = devices // 2
    lead = devices // 16
    planes = reach // PLANE + 2
    kept = (reach + lead + 1) * rows
    freqs = np.power(THETA, -np.arange(0, HD, 2) / HD).astype(np.float32)
    freqs = jnp.asarray(np.concatenate([freqs, freqs])[None, :])
    vmem = pl.BlockSpec(memory_space=pltpu.VMEM)
    smem = pl.BlockSpec(memory_space=pltpu.SMEM)
    dma = pltpu.SemaphoreType.DMA
    return pl.pallas_call(
        functools.partial(kernel, devices, reach, lead),
        out_shape=(
            pltpu.VMEM(queries.shape, BF16),
            pltpu.VMEM((kept, 2 * keys.shape[1]), BF16),
        ),
        in_specs=[vmem] * 6 + [smem] * 3,
        out_specs=(vmem, vmem),
        scratch_shapes=[
            pltpu.VMEM((kv_heads, planes * PLANE * rows, 2 * HD), BF16),
            pltpu.VMEM((q_heads * rows, HD), BF16),
            pltpu.VMEM((rows, (reach + 1) * rows), F32),
            pltpu.VMEM((kept, HD), BF16),
            pltpu.VMEM((kv_heads, rows, group * HD), BF16),
            dma((STAGES, planes, PLANE)),
            dma((STAGES, planes, 5)),
            dma((kv_heads, TRADE)),
            dma((kv_heads, TRADE)),
            dma((kv_heads,)),
        ],
        compiler_params=pltpu.CompilerParams(
            collective_id=0, has_side_effects=True, vmem_limit_bytes=40 * 2**20
        ),
    )(
        queries, keys, values, q_gain[None, :], k_gain[None, :], freqs,
        lengths, placing, owners,
    )


def solution(mesh):
    return jax.shard_map(
        body,
        mesh=mesh,
        in_specs=(
            P(("groups", "ctx"), None),
            P(("groups", "ctx"), None),
            P(("groups", "ctx"), None),
            P(),
            P(),
            P("groups"),
            P(("groups", "ctx"), None),
            P("groups"),
        ),
        out_specs=(P(("groups", "ctx"), None), P(("groups", "ctx"), None)),
        check_vma=False,
    )
```
